32 devices in a mesh: group: 2 (over x), env: 16 (over z, y, core).
Axes of the slice: x: 2, y: 2, z: 4, core: 2. Of those that a mesh axis runs over, the one named last changes fastest.
Arguments:
- descriptors: bfloat16 [16384, 1024], P(('group', 'env')), parts along dimension 0, may hold values from 0 to 32
- sparse_points: bfloat16 [25600, 1024], P(('group', 'env')), parts along dimension 0, may hold values from 0 to 32
- counts: int32 [32, 12], P(('group', 'env')), parts along dimension 0, may hold values from 1 to 128, 512 in all within a row
- energies: float32 [384], P(('group', 'env')), parts along dimension 0, may hold values from -0.75 to 0.75
Outputs:
- design: bfloat16 [384, 12800], P('group', 'env'), parts along dimension 0
- normal_rhs: float32 [25600], P(('group', 'env')), parts along dimension 0
The draws below stay inside these ranges and needn't reach their ends.
There are 2 independent parts, one for each index of `group`. The reference program is written for one: setup_inputs(seed, part) draws one part's arguments, and reference() takes and returns one part's arrays. A program takes and returns all parts, laid end to end along the dimension named above; each array names one. Nothing has to cross between parts.
All inputs are finite; a program needn't handle non-finite values.
Results may differ from the reference program's by a relative error of at most 0.0031.
Values may be sent and summed in bfloat16 or wider, within the bound.
A program may use at most 128 MiB of HBM per device.

```python
import math
import jax
import jax.numpy as jnp
import numpy as np
from jax import lax

D = 1024
S = 12800
A_DEV = 512
C_DEV = 12
ATOMS = 8192
CONFIGS = 192
N_ENV = 16


def cluster_centres(key):
    key_support, key_values = jax.random.split(key)
    support = jax.random.bernoulli(key_support, 0.25, (64, D))
    values = jnp.exp(jax.random.uniform(key_values, (64, D), jnp.float32, math.log(0.3), math.log(3.0)))
    return jnp.where(support, values, 0.0)


def mixed_rows(key, centres, rows, factors, noise):
    key_first, key_second, key_weight = jax.random.split(key, 3)
    first = jax.random.randint(key_first, (rows,), 0, 64)
    second = jax.random.randint(key_second, (rows,), 0, 64)
    weight = jax.random.uniform(key_weight, (rows, 1), jnp.float32, 0.0, 1.0)
    base = weight * centres[first] + (1.0 - weight) * centres[second]
    values = base * factors + noise
    return jnp.clip(values, 0.0, 32.0).astype(jnp.bfloat16)


def draw_descriptors(key, part):
    centres = cluster_centres(key)
    key = jax.random.fold_in(key, 11)
    key_mix, key_factor, key_noise = jax.random.split(key, 3)
    factors = jnp.exp(0.7 * jnp.clip(jax.random.normal(key_factor, (ATOMS, D), jnp.float32), -3.0, 3.0))
    noise = jax.random.uniform(key_noise, (ATOMS, D), jnp.float32, 0.0, 0.3)
    return mixed_rows(key_mix, centres, ATOMS, factors, noise)


def draw_sparse_points(key, part):
    centres = cluster_centres(key)
    key = jax.random.fold_in(key, 23)
    key_mix, key_factor, key_noise = jax.random.split(key, 3)
    factors = jnp.exp(0.7 * jnp.clip(jax.random.normal(key_factor, (S, D), jnp.float32), -3.0, 3.0))
    noise = jax.random.uniform(key_noise, (S, D), jnp.float32, 0.0, 0.3)
    return mixed_rows(key_mix, centres, S, factors, noise)


def steps_of(rng, extent, pieces, smallest, high):
    level, own = 1.0, jax.random.fold_in(rng, 6)
    for position, shards_of in pieces:
        draws = jnp.exp(jax.random.uniform(jax.random.fold_in(own, position), (shards_of,), jnp.float32, smallest / len(pieces), high / len(pieces)))
        level = level * jnp.repeat(draws, extent[position] // shards_of).reshape([-1 if axis == position else 1 for axis in range(len(extent))])
    return level


def profile(count, total, reach, slope):
    loads = [(1 << 20) // math.isqrt(grade ** slope) + 1 for grade in range(2, count + 1)]
    spare, given = total - reach - (count - 1), [1] * (count - 1)
    while spare > 0:
        free = [i for i in range(count - 1) if given[i] < reach]
        whole, remaining = sum([loads[i] for i in free]), spare
        for i in free:
            addition = min(reach - given[i], max(1, remaining * loads[i] // whole), spare)
            given[i] = given[i] + addition
            spare = spare - addition
    return np.array([reach] + given)


def uneven(own_key, number_of, total, most, skew):
    if number_of == 2:
        one = jax.random.randint(own_key, (), max(1, total - most), min(most, total - 1) + 1)
        return jnp.stack([one, total - one])
    tallies = jnp.asarray(profile(number_of, total, most, skew), jnp.int32)
    pairs = (number_of - 1) // 2
    source_of, sink = tallies[1:1 + 2 * pairs:2], tallies[2:2 + 2 * pairs:2]
    margin = jnp.minimum(source_of - 1, most - sink)
    shifted = jax.random.randint(jax.random.fold_in(own_key, 1), (pairs,), 0, 1 << 20) % (margin + 1)
    tallies = tallies.at[1:1 + 2 * pairs:2].set(source_of - shifted).at[2:2 + 2 * pairs:2].set(sink + shifted)
    return tallies[jax.random.permutation(jax.random.fold_in(own_key, 2), number_of)]


def centred(stream_key, dims, deviation, bound, cuts=(), held_as=jnp.bfloat16):
    result = jax.random.normal(stream_key, dims, jnp.float32) * deviation
    if len(cuts) > 0:
        result = steps_of(stream_key, dims, cuts, -0.22, 0.18) * result
    return jnp.clip(result, min=-bound, max=bound).astype(held_as)


def setup_inputs(seed: int = 0, part: int = 0) -> dict:
    seeds = jax.random.split(jax.random.key(seed), 5)
    part_splits = jax.random.split(jax.random.fold_in(seeds[4], part), 5)
    descriptors = draw_descriptors(jax.random.fold_in(jax.random.fold_in(seeds[4], part), 71), part)
    sparse_points = draw_sparse_points(jax.random.fold_in(jax.random.fold_in(seeds[4], part), 71), part)
    counts = jax.vmap(lambda own: uneven(own, C_DEV, A_DEV, A_DEV // 4, 2))(jax.random.split(part_splits[2], N_ENV)).reshape((N_ENV, C_DEV)).astype(jnp.int32)
    energies = centred(part_splits[3], (CONFIGS,), 0.05, 0.75, ((0, 16),), jnp.float32)
    return {"descriptors": descriptors, "sparse_points": sparse_points, "counts": counts, "energies": energies}


EPS = 1e-06

def reference(descriptors, sparse_points, counts, energies):
    sparse_f = sparse_points.astype(jnp.float32)
    inv_sparse = lax.rsqrt(lax.optimization_barrier(jnp.sum(sparse_f * sparse_f, axis=1)) + EPS)
    blocks = descriptors.reshape(N_ENV, A_DEV, D)

    def one_block(inputs):
        block_rows, block_counts = inputs
        rows_f = block_rows.astype(jnp.float32)
        inv_atoms = lax.rsqrt(lax.optimization_barrier(jnp.sum(rows_f * rows_f, axis=1)) + EPS)
        products = jnp.dot(block_rows, sparse_points.T, preferred_element_type=jnp.float32)
        cosine = products * inv_atoms[:, None] * inv_sparse[None, :]
        squared = cosine * cosine
        kernel = squared * squared
        seg_ends = jnp.cumsum(block_counts).astype(jnp.int32)
        positions = jnp.arange(A_DEV, dtype=jnp.int32)
        config_ids = lax.optimization_barrier(jnp.sum((positions[:, None] >= seg_ends[None, :]).astype(jnp.int32), axis=1))
        return jax.ops.segment_sum(kernel, config_ids, num_segments=C_DEV)
    sums = lax.map(one_block, (blocks, counts))
    design = sums.reshape(CONFIGS, S).astype(jnp.bfloat16)
    normal_rhs = jnp.dot(energies, design.astype(jnp.float32), precision=lax.Precision.HIGHEST)
    return (design, normal_rhs)
```

```python
import functools

import jax
import jax.numpy as jnp
from jax import lax
from jax.experimental import pallas as pl
from jax.experimental.pallas import tpu as pltpu
from jax.sharding import PartitionSpec as P

EPS = 1e-06
LANES = 128
VMEM_BUDGET = 44 * 1024 * 1024


def inverse_norms(values):
    values_f = values.astype(jnp.float32)
    return lax.rsqrt(jnp.sum(values_f * values_f, axis=1) + EPS)


def kernel_block(atom_rows, inv_atoms, sparse_rows, inv_sparse):
    products = lax.dot_general(
        atom_rows, sparse_rows, (((1,), (1,)), ((), ())), preferred_element_type=jnp.float32
    )
    cosine = products * inv_atoms[:, None] * inv_sparse[None, :]
    squared = cosine * cosine
    return squared * squared


def gather_sparse(descriptors, sparse_points, counts, energies):
    atoms_here = descriptors.shape[0]
    all_energies = lax.all_gather(energies, "env", axis=0, tiled=True)
    inv_atoms = inverse_norms(descriptors)
    seg_ends = jnp.cumsum(counts[0])
    seg_starts = seg_ends - counts[0]
    positions = jnp.arange(atoms_here, dtype=jnp.int32)
    onehot = (
        (positions[None, :] >= seg_starts[:, None]) & (positions[None, :] < seg_ends[:, None])
    ).astype(jnp.float32)
    block_rows = lax.all_gather(sparse_points, "env", axis=0, tiled=True)
    inv_sparse = inverse_norms(block_rows)
    kernel = kernel_block(descriptors, inv_atoms, block_rows, inv_sparse)
    config_part = jnp.dot(onehot, kernel, precision=lax.Precision.HIGHEST)
    design = lax.all_to_all(
        config_part.astype(jnp.bfloat16), "env", split_axis=1, concat_axis=0, tiled=True
    )
    normal_rhs = jnp.dot(all_energies, design.astype(jnp.float32), precision=lax.Precision.HIGHEST)
    return (design, normal_rhs)


def ring_kernel(
    n_env, chunks, a_hbm, s_hbm, counts_ref, energies_ref, design_ref, rhs_ref,
    blocks, s_ref, metas, inv_s, sums, rhs_acc,
    own_sem, sparse_sem, send_next, send_side, recv_next, recv_side,
    meta_send_next, meta_send_side, meta_recv_next, meta_recv_side,
):
    ring = n_env // 2
    column = ring // 2
    n_atoms, depth = a_hbm.shape
    n_sparse = s_ref.shape[0]
    n_conf = counts_ref.shape[1]
    rows = n_atoms // chunks

    me = lax.axis_index("env")
    core = me % 2
    y = (me // 2) % 2
    z = me // 4
    place = z * (1 - y) + (2 * column - 1 - z) * y
    step_way = 1 - 2 * core

    def device_at(p, c):
        py = p // column
        pz = p * (1 - py) + (2 * column - 1 - p) * py
        return pz * 4 + py * 2 + c

    nxt = device_at((place + step_way + ring) % ring, core)
    prv = device_at((place - step_way + ring) % ring, core)
    side = me + 1 - 2 * core

    barrier = pltpu.get_barrier_semaphore()
    for other in (nxt, prv, side):
        pl.semaphore_signal(
            barrier, inc=1, device_id={"env": other}, device_id_type=pl.DeviceIdType.MESH
        )

    own = [
        pltpu.make_async_copy(
            a_hbm.at[pl.ds(j * rows, rows)], blocks.at[0, pl.ds(j * rows, rows)], own_sem.at[j]
        )
        for j in range(chunks)
    ]
    for copy in own:
        copy.start()
    sparse = pltpu.make_async_copy(s_hbm, s_ref, sparse_sem)
    sparse.start()

    def remote(src, dst, send, recv, device):
        return pltpu.make_async_remote_copy(
            src_ref=src, dst_ref=dst, send_sem=send, recv_sem=recv,
            device_id={"env": device}, device_id_type=pl.DeviceIdType.MESH,
        )

    def piece(k, j):
        return blocks.at[k, pl.ds(j * rows, rows)]

    def to_next(k, j):
        return remote(piece(k, j), piece(k + 1, j), send_next.at[k, j], recv_next.at[k + 1, j], nxt)

    def to_side(k, j):
        return remote(piece(k, j), piece(ring + k, j), send_side.at[k, j], recv_side.at[k, j], side)

    def meta_next(k):
        return remote(metas.at[k], metas.at[k + 1], meta_send_next.at[k], meta_recv_next.at[k + 1], nxt)

    def meta_side(k):
        return remote(metas.at[k], metas.at[ring + k], meta_send_side.at[k], meta_recv_side.at[k], side)

    pl.semaphore_wait(barrier, 3)
    for j in range(chunks):
        own[j].wait()
        to_next(0, j).start()
        to_side(0, j).start()

    ones = jnp.ones((8, depth), jnp.bfloat16)
    for j in range(chunks):
        values = blocks[0, j * rows:(j + 1) * rows, :].astype(jnp.float32)
        squares = values * values
        high = squares.astype(jnp.bfloat16)
        low = (squares - high.astype(jnp.float32)).astype(jnp.bfloat16)
        contract = (((1,), (1,)), ((), ()))
        total = lax.dot_general(ones, high, contract, preferred_element_type=jnp.float32)
        total += lax.dot_general(ones, low, contract, preferred_element_type=jnp.float32)
        metas[0, :, j * rows:(j + 1) * rows] = lax.rsqrt(total + EPS)
    padded = jnp.concatenate(
        [counts_ref[...].astype(jnp.float32), jnp.zeros((1, LANES - n_conf), jnp.float32)], axis=1
    )
    lower = lax.broadcasted_iota(jnp.int32, (LANES, LANES), 0)
    upper = lax.broadcasted_iota(jnp.int32, (LANES, LANES), 1)
    ends = jnp.dot(
        jnp.broadcast_to(padded, (8, LANES)).astype(jnp.bfloat16),
        (lower <= upper).astype(jnp.bfloat16),
        preferred_element_type=jnp.float32,
    )[0:1]
    metas[0, 1:2, 0:LANES] = ends - padded
    metas[0, 2:3, 0:LANES] = ends
    metas[0, 3:4, 0:LANES] = jnp.concatenate(
        [energies_ref[...], jnp.zeros((1, LANES - n_conf), jnp.float32)], axis=1
    )
    meta_next(0).start()
    meta_side(0).start()

    sparse.wait()
    values = s_ref[...].astype(jnp.float32)
    norms = lax.rsqrt(jnp.sum(values * values, axis=1, keepdims=True) + EPS)
    inv_s[...] = jnp.broadcast_to(norms, inv_s.shape)
    rhs_acc[...] = jnp.zeros_like(rhs_acc)
    sums[...] = jnp.zeros_like(sums)

    def part(way, slot, j):
        products = lax.dot_general(
            s_ref[...], blocks[slot, j * rows:(j + 1) * rows, :], (((1,), (1,)), ((), ())),
            preferred_element_type=jnp.float32,
        )
        cosine = products * metas[slot, 0:1, j * rows:(j + 1) * rows] * inv_s[:, 0:1]
        squared = cosine * cosine
        kernel = squared * squared
        high = kernel.astype(jnp.bfloat16)
        low = (kernel - high.astype(jnp.float32)).astype(jnp.bfloat16)
        at = (lax.broadcasted_iota(jnp.int32, (rows, LANES), 0) + j * rows).astype(jnp.float32)
        inside = (at >= metas[slot, 1:2, 0:LANES]) & (at < metas[slot, 2:3, 0:LANES])
        onehot = jnp.where(inside, 1.0, 0.0).astype(jnp.bfloat16)
        total = jnp.dot(high, onehot, preferred_element_type=jnp.float32)
        total += jnp.dot(low, onehot, preferred_element_type=jnp.float32)
        if j == 0:
            sums[way, 0:n_sparse] = total
        else:
            sums[way, 0:n_sparse] += total

    def finish(way, slot, source):
        rounded = sums[way].astype(jnp.bfloat16).astype(jnp.float32)
        rhs_acc[...] += rounded * metas[slot, 3:4, 0:LANES]
        turned = rounded.T[0:n_conf, 0:n_sparse]
        design_ref[source] = turned.astype(jnp.bfloat16)

    def own_source(k):
        return device_at((place + ring * ring - k * step_way) % ring, core)

    def side_source(k):
        return device_at((place + ring * ring + k * step_way) % ring, 1 - core)

    def use(k, j):
        part(0, k, j)
        if j == 0:
            meta_side(k).wait_recv()
        to_side(k, j).wait_recv()
        part(1, ring + k, j)
        if j == chunks - 1:
            finish(0, k, own_source(k))
            finish(1, ring + k, side_source(k))

    def step(k, last):
        for j in range(chunks):
            to_next(k - 1, j).wait_recv()
            if not last:
                to_next(k, j).start()
            to_side(k, j).start()
            if j == 0:
                meta_next(k - 1).wait_recv()
                if not last:
                    meta_next(k).start()
                meta_side(k).start()
                use(k - 1, chunks - 1)
            else:
                use(k, j - 1)

    for j in range(chunks - 1):
        use(0, j)

    @pl.loop(1, ring - 1)
    def _(k):
        step(k, False)

    step(ring - 1, True)
    use(ring - 1, chunks - 1)
    rhs_ref[...] = jnp.sum(rhs_acc[...].T, axis=0, keepdims=True)[:, 0:n_sparse]

    @pl.loop(0, ring)
    def _(k):
        for j in range(chunks):
            to_side(k, j).wait_send()
        meta_side(k).wait_send()

    @pl.loop(0, ring - 1)
    def _(k):
        for j in range(chunks):
            to_next(k, j).wait_send()
        meta_next(k).wait_send()


def gather_atoms(n_env, descriptors, sparse_points, counts, energies):
    n_atoms, depth = descriptors.shape
    n_sparse = sparse_points.shape[0]
    n_conf = counts.shape[1]
    ring = n_env // 2
    chunks = 2
    wide = pl.cdiv(n_sparse, LANES) * LANES
    dma = pltpu.SemaphoreType.DMA
    design, rhs = pl.pallas_call(
        functools.partial(ring_kernel, n_env, chunks),
        out_shape=(
            jax.ShapeDtypeStruct((n_env, n_conf, n_sparse), jnp.bfloat16),
            jax.ShapeDtypeStruct((1, n_sparse), jnp.float32),
        ),
        in_specs=[
            pl.BlockSpec(memory_space=pl.ANY),
            pl.BlockSpec(memory_space=pl.ANY),
            pl.BlockSpec(memory_space=pltpu.VMEM),
            pl.BlockSpec(memory_space=pltpu.VMEM),
        ],
        out_specs=(
            pl.BlockSpec(memory_space=pltpu.VMEM),
            pl.BlockSpec(memory_space=pltpu.VMEM),
        ),
        scratch_shapes=[
            pltpu.VMEM((n_env, n_atoms, depth), jnp.bfloat16),
            pltpu.VMEM((n_sparse, depth), jnp.bfloat16),
            pltpu.VMEM((n_env, 8, n_atoms), jnp.float32),
            pltpu.VMEM((n_sparse, LANES), jnp.float32),
            pltpu.VMEM((2, wide, LANES), jnp.float32),
            pltpu.VMEM((wide, LANES), jnp.float32),
            dma((chunks,)),
            dma,
            dma((ring, chunks)),
            dma((ring, chunks)),
            dma((ring, chunks)),
            dma((ring, chunks)),
            dma((ring,)),
            dma((ring,)),
            dma((ring,)),
            dma((ring,)),
        ],
        compiler_params=pltpu.CompilerParams(
            collective_id=0, has_side_effects=True, vmem_limit_bytes=VMEM_BUDGET
        ),
        cost_estimate=pl.CostEstimate(
            flops=2 * n_env * n_atoms * n_sparse * depth,
            bytes_accessed=2 * (n_atoms + n_sparse) * depth,
            transcendentals=0,
        ),
    )(descriptors, sparse_points, counts, energies.reshape(1, n_conf))
    return (design.reshape(n_env * n_conf, n_sparse), rhs.reshape(n_sparse))


def solution(mesh):
    n_env = mesh.shape["env"]

    def on_device(descriptors, sparse_points, counts, energies):
        gathered = 2 * n_env * descriptors.shape[0] * descriptors.shape[1]
        if n_env % 4 == 0 and n_env > 4 and gathered <= VMEM_BUDGET // 2:
            return gather_atoms(n_env, descriptors, sparse_points, counts, energies)
        return gather_sparse(descriptors, sparse_points, counts, energies)

    return jax.shard_map(
        on_device,
        mesh=mesh,
        in_specs=(
            P(("group", "env"), None),
            P(("group", "env"), None),
            P(("group", "env"), None),
            P(("group", "env")),
        ),
        out_specs=(P("group", "env"), P(("group", "env"))),
        check_vma=False,
    )
```

```python
import functools

import jax
import jax.numpy as jnp
from jax import lax
from jax.experimental import pallas as pl
from jax.experimental.pallas import tpu as pltpu
from jax.sharding import PartitionSpec as P

EPS = 1e-06
LANES = 128
VMEM_BUDGET = 44 * 1024 * 1024


def inverse_norms(values):
    values_f = values.astype(jnp.float32)
    return lax.rsqrt(jnp.sum(values_f * values_f, axis=1) + EPS)


def kernel_block(atom_rows, inv_atoms, sparse_rows, inv_sparse):
    products = lax.dot_general(
        atom_rows, sparse_rows, (((1,), (1,)), ((), ())), preferred_element_type=jnp.float32
    )
    cosine = products * inv_atoms[:, None] * inv_sparse[None, :]
    squared = cosine * cosine
    return squared * squared


def gather_sparse(descriptors, sparse_points, counts, energies):
    atoms_here = descriptors.shape[0]
    all_energies = lax.all_gather(energies, "env", axis=0, tiled=True)
    inv_atoms = inverse_norms(descriptors)
    seg_ends = jnp.cumsum(counts[0])
    seg_starts = seg_ends - counts[0]
    positions = jnp.arange(atoms_here, dtype=jnp.int32)
    onehot = (
        (positions[None, :] >= seg_starts[:, None]) & (positions[None, :] < seg_ends[:, None])
    ).astype(jnp.float32)
    block_rows = lax.all_gather(sparse_points, "env", axis=0, tiled=True)
    inv_sparse = inverse_norms(block_rows)
    kernel = kernel_block(descriptors, inv_atoms, block_rows, inv_sparse)
    config_part = jnp.dot(onehot, kernel, precision=lax.Precision.HIGHEST)
    design = lax.all_to_all(
        config_part.astype(jnp.bfloat16), "env", split_axis=1, concat_axis=0, tiled=True
    )
    normal_rhs = jnp.dot(all_energies, design.astype(jnp.float32), precision=lax.Precision.HIGHEST)
    return (design, normal_rhs)


def block_kernel(
    cuts, chunks, a_hbm, s_hbm, counts_hbm, energies_hbm, design_ref, rhs_ref,
    blocks, metas, sparse, other, inv_own, inv_other, sum_own, sum_other, out_other, in_other,
    row_energies, counts_ref, energies_ref,
    own_sem, small_sem, recv, send_y, send_side, send_part, send_cross,
    s_send, s_recv, r_send, r_recv, e_send, e_recv,
):
    n_atoms, depth = a_hbm.shape
    n_sparse = s_hbm.shape[0]
    n_conf = counts_hbm.shape[1]
    rows = n_atoms // chunks
    half = n_atoms // 2
    META = chunks
    items = [0, META] + list(range(1, chunks))

    me = lax.axis_index("env")
    core = me % 2
    y = (me // 2) % 2
    z = me // 4
    inner_i = (z % 3 + 1) // 2
    inner = inner_i == 1
    outer = inner_i == 0
    pair_z = z + 1 - 2 * (z % 2)
    side = me + 1 - 2 * core
    over = me + 2 - 4 * y
    partner = pair_z * 4 + y * 2 + core
    cross = (3 - z) * 4 + y * 2 + core
    own = 9 * inner_i

    barrier = pltpu.get_barrier_semaphore()

    def greet(device):
        pl.semaphore_signal(
            barrier, inc=1, device_id={"env": device}, device_id_type=pl.DeviceIdType.MESH
        )

    for device in (side, over, partner):
        greet(device)

    @pl.when(inner)
    def _():
        greet(cross)

    def piece(slot, item):
        if item == META:
            return metas.at[slot]
        return blocks.at[slot, pl.ds(item * rows, rows)]

    def remote(src, dst, send, arrive, device):
        return pltpu.make_async_remote_copy(
            src_ref=src, dst_ref=dst, send_sem=send, recv_sem=arrive,
            device_id={"env": device}, device_id_type=pl.DeviceIdType.MESH,
        )

    def hand(src, dst, item, send, device):
        return remote(piece(src, item), piece(dst, item), send.at[item], recv.at[dst, item], device)

    def to_side(q, item):
        return hand(q, 4 + q, item, send_side.at[q], side)

    def to_over(q, item):
        return hand(q, q + 1, item, send_y.at[q // 2], over)

    def to_part(item):
        return hand(own, 8 - 6 * inner_i, item, send_part, partner)

    def to_cross(src, dst, item):
        return hand(src, dst, item, send_cross.at[dst // 2], cross)

    def arrived(slot, item):
        remote(
            piece(slot, item), piece(slot, item), send_part.at[item], recv.at[slot, item], side
        ).wait_recv()

    def s_rows(n):
        return pl.ds(cuts[n], cuts[n + 1] - cuts[n])

    def give_sparse(n):
        return remote(s_hbm.at[s_rows(n)], other.at[s_rows(n)], s_send.at[n], s_recv.at[n], partner)

    def give_sums(n):
        return remote(
            out_other.at[s_rows(n)], in_other.at[s_rows(n)], r_send.at[n], r_recv.at[n], partner
        )

    give_energies = remote(row_energies.at[0], row_energies.at[1], e_send, e_recv, partner)

    local = [
        pltpu.make_async_copy(a_hbm.at[pl.ds(j * rows, rows)], piece(own, j), own_sem.at[j])
        for j in range(chunks)
    ]
    local_sparse = pltpu.make_async_copy(s_hbm, sparse, small_sem.at[0])
    local_counts = pltpu.make_async_copy(counts_hbm, counts_ref, small_sem.at[1])
    local_energies = pltpu.make_async_copy(energies_hbm, energies_ref, small_sem.at[2])
    for copy in local + [local_counts, local_energies, local_sparse]:
        copy.start()

    def send_own(item):
        to_part(item).start()

        @pl.when(inner)
        def _():
            to_cross(own, 0, item).start()

        @pl.when(outer)
        def _():
            to_over(0, item).start()
            to_side(0, item).start()

    pl.semaphore_wait(barrier, 3 + inner_i)
    local[0].wait()
    send_own(0)

    for copy in local[1:]:
        copy.wait()
    ones = jnp.ones((8, depth), jnp.bfloat16)
    contract = (((1,), (1,)), ((), ()))
    for j in range(2):
        values = blocks[own, j * half:(j + 1) * half, :].astype(jnp.float32)
        squares = values * values
        high = squares.astype(jnp.bfloat16)
        low = (squares - high.astype(jnp.float32)).astype(jnp.bfloat16)
        total = lax.dot_general(ones, high, contract, preferred_element_type=jnp.float32)
        total += lax.dot_general(ones, low, contract, preferred_element_type=jnp.float32)
        metas[own, :, j * half:(j + 1) * half] = lax.rsqrt(total + EPS)
    local_counts.wait()
    local_energies.wait()
    down = lax.broadcasted_iota(jnp.int32, (LANES, LANES), 0)
    along = lax.broadcasted_iota(jnp.int32, (LANES, LANES), 1) % 16
    blank = jnp.zeros((1, LANES - n_conf), jnp.float32)

    def spread(row, keep):
        keep = jnp.where(keep & (along < n_conf), 1.0, 0.0)
        return jnp.dot(
            jnp.broadcast_to(jnp.concatenate([row, blank], axis=1), (8, LANES)), keep,
            precision=lax.Precision.HIGHEST, preferred_element_type=jnp.float32,
        )[0:1]

    counts_f = counts_ref[...].astype(jnp.float32)
    metas[own, 1:2, 0:LANES] = spread(counts_f, down < along)
    metas[own, 2:3, 0:LANES] = spread(counts_f, down <= along)
    metas[own, 3:4, 0:LANES] = spread(energies_ref[...], down == along)
    for item in items[1:]:
        send_own(item)

    def scale_rows(points, inv, start, stop):
        values = points[start:stop, :].astype(jnp.float32)
        norms = lax.rsqrt(jnp.sum(values * values, axis=1, keepdims=True) + EPS)
        inv[start:stop, :] = jnp.broadcast_to(norms, (stop - start, LANES))

    local_sparse.wait()
    scale_rows(sparse, inv_own, 0, n_sparse)
    sum_own[...] = jnp.zeros_like(sum_own)
    sum_other[...] = jnp.zeros_like(sum_other)
    if in_other.shape[0] > n_sparse:
        in_other[n_sparse:, :] = jnp.zeros((in_other.shape[0] - n_sparse, LANES), jnp.bfloat16)

    def unit(points, inv, sums, start, stop, slot, u):
        products = lax.dot_general(
            points[start:stop, :], blocks[slot, u * half:(u + 1) * half, :], contract,
            preferred_element_type=jnp.float32,
        )
        cosine = products * metas[slot, 0:1, u * half:(u + 1) * half] * inv[start:stop, 0:1]
        squared = cosine * cosine
        kernel = squared * squared
        high = kernel.astype(jnp.bfloat16)
        low = (kernel - high.astype(jnp.float32)).astype(jnp.bfloat16)
        at = (lax.broadcasted_iota(jnp.int32, (half, LANES), 0) + u * half).astype(jnp.float32)
        lane = lax.broadcasted_iota(jnp.int32, (half, LANES), 1)
        inside = (at >= metas[slot, 1:2, 0:LANES]) & (at < metas[slot, 2:3, 0:LANES])
        onehot = jnp.where(inside & (lane // 16 == slot), 1.0, 0.0).astype(jnp.bfloat16)
        total = jnp.dot(high, onehot, preferred_element_type=jnp.float32)
        total += jnp.dot(low, onehot, preferred_element_type=jnp.float32)
        sums[start:stop, :] += total

    def use_own(qs, u):
        first, n = qs

        @pl.loop(0, 2 * n)
        def _(i):
            unit(sparse, inv_own, sum_own, 0, n_sparse, first + i // 2 + 4 * (i % 2), u)

    def use_other(part, qs):
        first, n = qs

        @pl.loop(0, 2 * n)
        def _(i):
            for u in range(2):
                unit(
                    other, inv_other, sum_other, cuts[part], cuts[part + 1],
                    first + i // 2 + 4 * (i % 2), u,
                )

    def take_sparse(part):
        give_sparse(part).wait_recv()
        scale_rows(other, inv_other, cuts[part], cuts[part + 1])

    def give_back(part):
        out_other[s_rows(part)] = sum_other[s_rows(part)].astype(jnp.bfloat16)
        give_sums(part).start()

    for item in items:
        @pl.when(inner)
        def _():
            arrived(0, item)
            to_over(0, item).start()
            to_side(0, item).start()
            arrived(8, item)
            to_cross(8, 2, item).start()

        @pl.when(outer)
        def _():
            arrived(2, item)
            to_over(2, item).start()
            to_side(2, item).start()

        arrived(1, item)
        to_side(1, item).start()
        arrived(4, item)
        arrived(5, item)
        if item == chunks // 2:
            give_sparse(0).start()
            use_own((0, 2), 0)
        if item == chunks - 1:
            give_sparse(1).start()

    for item in items:
        @pl.when(inner)
        def _():
            arrived(2, item)
            to_over(2, item).start()
            to_side(2, item).start()

        arrived(6, item)
        if item == chunks - 1:
            use_own((2, 1), 1)
            use_other(0, (2, 1))
            take_sparse(1)
            use_other(1, (0, 3))
        arrived(3, item)
        to_side(3, item).start()
        if item == 0:
            give_sparse(2).start()
            use_own((0, 2), 1)
        if item == 1:
            give_sparse(3).start()
            take_sparse(0)
            use_other(0, (0, 2))
        arrived(7, item)
        if item == chunks // 2:
            use_own((2, 2), 0)

    use_own((3, 1), 1)
    use_other(0, (3, 1))
    give_back(0)
    use_other(1, (3, 1))
    give_back(1)

    lanes = lax.broadcasted_iota(jnp.int32, (1, LANES), 1) // 16
    mine = jnp.zeros((1, LANES), jnp.float32)
    for slot in range(8):
        mine += jnp.where(lanes == slot, metas[slot, 3:4, 0:LANES], 0.0)
    row_energies[0] = jnp.broadcast_to(mine, (8, LANES))
    give_energies.start()

    def finish(rounded, energies, at_z, at_inner):
        other_z = at_z + 1 - 2 * (at_z % 2)
        near = at_z + at_inner * (3 - 2 * at_z)
        far = other_z + at_inner * (3 - 2 * other_z)
        turned = rounded.T
        for slot in range(8):
            q = slot % 4
            from_z = near if q < 2 else far
            from_y = y if q % 2 == 0 else 1 - y
            from_core = core if slot < 4 else 1 - core
            design_ref[from_z * 4 + from_y * 2 + from_core] = turned[
                16 * slot:16 * slot + n_conf, 0:n_sparse
            ].astype(jnp.bfloat16)
        return jnp.sum((rounded * energies).T, axis=0, keepdims=True)[:, 0:n_sparse]

    take_sparse(2)
    use_other(2, (0, 4))
    give_back(2)
    rhs_ref[...] = finish(
        sum_own[...].astype(jnp.bfloat16).astype(jnp.float32), mine, z, inner_i
    )
    take_sparse(3)
    use_other(3, (0, 4))
    give_back(3)

    give_energies.wait_recv()
    for part in range(len(cuts) - 1):
        give_sums(part).wait_recv()
    rhs_ref[...] += finish(
        in_other[...].astype(jnp.float32), row_energies[1, 0:1, :], pair_z, 1 - inner_i
    )

    give_energies.wait_send()
    for part in range(len(cuts) - 1):
        give_sparse(part).wait_send()
        give_sums(part).wait_send()
    for item in items:
        to_part(item).wait_send()
        for q in range(4):
            to_side(q, item).wait_send()
        to_over(0, item).wait_send()
        to_over(2, item).wait_send()

        @pl.when(inner)
        def _():
            to_cross(own, 0, item).wait_send()
            to_cross(8, 2, item).wait_send()


def split_both(descriptors, sparse_points, counts, energies):
    n_atoms, depth = descriptors.shape
    n_sparse = sparse_points.shape[0]
    n_conf = counts.shape[1]
    n_env = 16
    chunks = 4
    unit = n_sparse // 6 // LANES * LANES
    cuts = (0, 2 * unit, 4 * unit, 5 * unit, n_sparse)
    parts = len(cuts) - 1
    wide = pl.cdiv(n_sparse, LANES) * LANES
    dma = pltpu.SemaphoreType.DMA
    design, rhs = pl.pallas_call(
        functools.partial(block_kernel, cuts, chunks),
        out_shape=(
            jax.ShapeDtypeStruct((n_env, n_conf, n_sparse), jnp.bfloat16),
            jax.ShapeDtypeStruct((1, n_sparse), jnp.float32),
        ),
        in_specs=[pl.BlockSpec(memory_space=pltpu.HBM)] * 4,
        out_specs=(
            pl.BlockSpec(memory_space=pltpu.VMEM),
            pl.BlockSpec(memory_space=pltpu.VMEM),
        ),
        scratch_shapes=[
            pltpu.VMEM((10, n_atoms, depth), jnp.bfloat16),
            pltpu.VMEM((10, 8, n_atoms), jnp.float32),
            pltpu.VMEM((n_sparse, depth), jnp.bfloat16),
            pltpu.VMEM((n_sparse, depth), jnp.bfloat16),
            pltpu.VMEM((n_sparse, LANES), jnp.float32),
            pltpu.VMEM((n_sparse, LANES), jnp.float32),
            pltpu.VMEM((wide, LANES), jnp.float32),
            pltpu.VMEM((wide, LANES), jnp.float32),
            pltpu.VMEM((n_sparse, LANES), jnp.bfloat16),
            pltpu.VMEM((wide, LANES), jnp.bfloat16),
            pltpu.VMEM((2, 8, LANES), jnp.float32),
            pltpu.VMEM((1, n_conf), jnp.int32),
            pltpu.VMEM((1, n_conf), jnp.float32),
            dma((chunks,)),
            dma((3,)),
            dma((9, chunks + 1)),
            dma((2, chunks + 1)),
            dma((4, chunks + 1)),
            dma((chunks + 1,)),
            dma((2, chunks + 1)),
            dma((parts,)),
            dma((parts,)),
            dma((parts,)),
            dma((parts,)),
            dma,
            dma,
        ],
        compiler_params=pltpu.CompilerParams(
            collective_id=0, has_side_effects=True, vmem_limit_bytes=VMEM_BUDGET
        ),
        cost_estimate=pl.CostEstimate(
            flops=2 * n_env * n_atoms * n_sparse * depth,
            bytes_accessed=2 * (n_atoms + n_sparse) * depth,
            transcendentals=0,
        ),
    )(descriptors, sparse_points, counts, energies.reshape(1, n_conf))
    return (design.reshape(n_env * n_conf, n_sparse), rhs.reshape(n_sparse))


def solution(mesh):
    n_env = mesh.shape["env"]

    def on_device(descriptors, sparse_points, counts, energies):
        if n_env == 16 and counts.shape[1] <= 16 and sparse_points.shape[0] >= 6 * LANES:
            return split_both(descriptors, sparse_points, counts, energies)
        return gather_sparse(descriptors, sparse_points, counts, energies)

    return jax.shard_map(
        on_device,
        mesh=mesh,
        in_specs=(
            P(("group", "env"), None),
            P(("group", "env"), None),
            P(("group", "env"), None),
            P(("group", "env")),
        ),
        out_specs=(P("group", "env"), P(("group", "env"))),
        check_vma=False,
    )
```

```python
import functools

import jax
import jax.numpy as jnp
from jax import lax
from jax.experimental import pallas as pl
from jax.experimental.pallas import tpu as pltpu
from jax.sharding import PartitionSpec as P

EPS = 1e-06
LANES = 128
VMEM_BUDGET = 44 * 1024 * 1024


def inverse_norms(values):
    values_f = values.astype(jnp.float32)
    return lax.rsqrt(jnp.sum(values_f * values_f, axis=1) + EPS)


def kernel_block(atom_rows, inv_atoms, sparse_rows, inv_sparse):
    products = lax.dot_general(
        atom_rows, sparse_rows, (((1,), (1,)), ((), ())), preferred_element_type=jnp.float32
    )
    cosine = products * inv_atoms[:, None] * inv_sparse[None, :]
    squared = cosine * cosine
    return squared * squared


def gather_sparse(descriptors, sparse_points, counts, energies):
    atoms_here = descriptors.shape[0]
    all_energies = lax.all_gather(energies, "env", axis=0, tiled=True)
    inv_atoms = inverse_norms(descriptors)
    seg_ends = jnp.cumsum(counts[0])
    seg_starts = seg_ends - counts[0]
    positions = jnp.arange(atoms_here, dtype=jnp.int32)
    onehot = (
        (positions[None, :] >= seg_starts[:, None]) & (positions[None, :] < seg_ends[:, None])
    ).astype(jnp.float32)
    block_rows = lax.all_gather(sparse_points, "env", axis=0, tiled=True)
    inv_sparse = inverse_norms(block_rows)
    kernel = kernel_block(descriptors, inv_atoms, block_rows, inv_sparse)
    config_part = jnp.dot(onehot, kernel, precision=lax.Precision.HIGHEST)
    design = lax.all_to_all(
        config_part.astype(jnp.bfloat16), "env", split_axis=1, concat_axis=0, tiled=True
    )
    normal_rhs = jnp.dot(all_energies, design.astype(jnp.float32), precision=lax.Precision.HIGHEST)
    return (design, normal_rhs)


def block_kernel(
    cuts, chunks, a_hbm, s_hbm, counts_hbm, energies_hbm, design_ref, rhs_ref,
    blocks, metas, sparse, other, inv_own, inv_other, sum_own, sum_other, out_other, in_other,
    row_energies, counts_ref, energies_ref,
    own_sem, small_sem, recv, send_y, send_side, send_part, send_cross,
    s_send, s_recv, r_send, r_recv, e_send, e_recv,
):
    n_atoms, depth = a_hbm.shape
    n_sparse = s_hbm.shape[0]
    n_conf = counts_hbm.shape[1]
    rows = n_atoms // chunks
    half = n_atoms // 2
    META = chunks
    items = [0, META] + list(range(1, chunks))
    last = chunks - 1

    me = lax.axis_index("env")
    core = me % 2
    y = (me // 2) % 2
    z = me // 4
    inner_i = (z % 3 + 1) // 2
    inner = inner_i == 1
    outer = inner_i == 0
    pair_z = z + 1 - 2 * (z % 2)
    side = me + 1 - 2 * core
    over = me + 2 - 4 * y
    partner = pair_z * 4 + y * 2 + core
    cross = (3 - z) * 4 + y * 2 + core
    own = 9 * inner_i

    barrier = pltpu.get_barrier_semaphore()

    def greet(device):
        pl.semaphore_signal(
            barrier, inc=1, device_id={"env": device}, device_id_type=pl.DeviceIdType.MESH
        )

    for device in (side, over, partner):
        greet(device)

    @pl.when(inner)
    def _():
        greet(cross)

    def piece(slot, item):
        if item == META:
            return metas.at[slot]
        return blocks.at[slot, pl.ds(item * rows, rows)]

    def remote(src, dst, send, arrive, device):
        return pltpu.make_async_remote_copy(
            src_ref=src, dst_ref=dst, send_sem=send, recv_sem=arrive,
            device_id={"env": device}, device_id_type=pl.DeviceIdType.MESH,
        )

    def hand(src, dst, item, send, device):
        return remote(piece(src, item), piece(dst, item), send.at[item], recv.at[dst, item], device)

    def to_side(q, item):
        return hand(q, 4 + q, item, send_side.at[q], side)

    def to_over(q, item):
        return hand(q, q + 1, item, send_y.at[q // 2], over)

    def to_part(item):
        return hand(own, 8 - 6 * inner_i, item, send_part, partner)

    def to_cross(src, dst, item):
        return hand(src, dst, item, send_cross.at[dst // 2], cross)

    def arrived(slot, item):
        remote(
            piece(slot, item), piece(slot, item), send_part.at[item], recv.at[slot, item], side
        ).wait_recv()

    def s_rows(n):
        return pl.ds(cuts[n], cuts[n + 1] - cuts[n])

    def give_sparse(n):
        return remote(s_hbm.at[s_rows(n)], other.at[s_rows(n)], s_send.at[n], s_recv.at[n], partner)

    def give_sums(n):
        return remote(
            out_other.at[s_rows(n)], in_other.at[s_rows(n)], r_send.at[n], r_recv.at[n], partner
        )

    give_energies = remote(row_energies.at[0], row_energies.at[1], e_send, e_recv, partner)

    local = [
        pltpu.make_async_copy(a_hbm.at[pl.ds(j * rows, rows)], piece(own, j), own_sem.at[j])
        for j in range(chunks)
    ]
    local_sparse = pltpu.make_async_copy(s_hbm, sparse, small_sem.at[0])
    local_counts = pltpu.make_async_copy(counts_hbm, counts_ref, small_sem.at[1])
    local_energies = pltpu.make_async_copy(energies_hbm, energies_ref, small_sem.at[2])
    for copy in local + [local_counts, local_energies, local_sparse]:
        copy.start()

    def send_own(item):
        to_part(item).start()

        @pl.when(inner)
        def _():
            to_cross(own, 0, item).start()

        @pl.when(outer)
        def _():
            to_over(0, item).start()
            to_side(0, item).start()

    pl.semaphore_wait(barrier, 3 + inner_i)
    local[0].wait()
    send_own(0)

    for copy in local[1:]:
        copy.wait()
    ones = jnp.ones((8, depth), jnp.bfloat16)
    contract = (((1,), (1,)), ((), ()))
    for j in range(2):
        values = blocks[own, j * half:(j + 1) * half, :].astype(jnp.float32)
        squares = values * values
        high = squares.astype(jnp.bfloat16)
        low = (squares - high.astype(jnp.float32)).astype(jnp.bfloat16)
        total = lax.dot_general(ones, high, contract, preferred_element_type=jnp.float32)
        total += lax.dot_general(ones, low, contract, preferred_element_type=jnp.float32)
        metas[own, :, j * half:(j + 1) * half] = lax.rsqrt(total + EPS)
    local_counts.wait()
    local_energies.wait()
    down = lax.broadcasted_iota(jnp.int32, (LANES, LANES), 0)
    along = lax.broadcasted_iota(jnp.int32, (LANES, LANES), 1) % 16
    blank = jnp.zeros((1, LANES - n_conf), jnp.float32)

    def spread(row, keep):
        keep = jnp.where(keep & (along < n_conf), 1.0, 0.0)
        return jnp.dot(
            jnp.broadcast_to(jnp.concatenate([row, blank], axis=1), (8, LANES)), keep,
            precision=lax.Precision.HIGHEST, preferred_element_type=jnp.float32,
        )[0:1]

    counts_f = counts_ref[...].astype(jnp.float32)
    metas[own, 1:2, 0:LANES] = spread(counts_f, down < along)
    metas[own, 2:3, 0:LANES] = spread(counts_f, down <= along)
    metas[own, 3:4, 0:LANES] = spread(energies_ref[...], down == along)
    send_own(META)
    send_own(1)

    def scale_rows(points, inv, start, stop):
        values = points[start:stop, :].astype(jnp.float32)
        norms = lax.rsqrt(jnp.sum(values * values, axis=1, keepdims=True) + EPS)
        inv[start:stop, :] = jnp.broadcast_to(norms, (stop - start, LANES))

    local_sparse.wait()
    scale_rows(sparse, inv_own, 0, n_sparse)
    sum_own[...] = jnp.zeros_like(sum_own)
    sum_other[...] = jnp.zeros_like(sum_other)
    if in_other.shape[0] > n_sparse:
        in_other[n_sparse:, :] = jnp.zeros((in_other.shape[0] - n_sparse, LANES), jnp.bfloat16)

    def unit(points, inv, sums, start, stop, slot, first, end):
        products = lax.dot_general(
            points[start:stop, :], blocks[slot, first:end, :], contract,
            preferred_element_type=jnp.float32,
        )
        scale = jnp.concatenate([inv[start:stop, :]] * ((end - first) // LANES), axis=1)
        cosine = products * metas[slot, 0:1, first:end] * scale
        squared = cosine * cosine
        kernel = squared * squared
        high = kernel.astype(jnp.bfloat16)
        low = (kernel - high.astype(jnp.float32)).astype(jnp.bfloat16)
        at = (lax.broadcasted_iota(jnp.int32, (end - first, LANES), 0) + first).astype(jnp.float32)
        lane = lax.broadcasted_iota(jnp.int32, (end - first, LANES), 1)
        inside = (at >= metas[slot, 1:2, 0:LANES]) & (at < metas[slot, 2:3, 0:LANES])
        onehot = jnp.where(inside & (lane // 16 == slot), 1.0, 0.0).astype(jnp.bfloat16)
        total = jnp.dot(high, onehot, preferred_element_type=jnp.float32)
        total += jnp.dot(low, onehot, preferred_element_type=jnp.float32)
        sums[start:stop, :] += total

    def use_own(q, n, first=0, end=None):
        stop = n_atoms if end is None else end

        @pl.loop(0, 2 * n)
        def _(i):
            unit(sparse, inv_own, sum_own, 0, n_sparse, q + i // 2 + 4 * (i % 2), first, stop)

    def use_other(part, upto, q, n):
        @pl.loop(0, 2 * n)
        def _(i):
            unit(
                other, inv_other, sum_other, cuts[part], cuts[upto], q + i // 2 + 4 * (i % 2),
                0, n_atoms,
            )

    def take_sparse(part):
        give_sparse(part).wait_recv()
        scale_rows(other, inv_other, cuts[part], cuts[part + 1])

    def give_back(part):
        out_other[s_rows(part)] = sum_other[s_rows(part)].astype(jnp.bfloat16)
        give_sums(part).start()

    def items_of(j):
        return [0, META] if j == 0 else [j]

    def second_wave(j):
        for item in items_of(j):
            @pl.when(inner)
            def _():
                to_cross(8, 2, item).start()

            @pl.when(outer)
            def _():
                to_over(2, item).start()

    def pass_aside(q, j):
        for item in items_of(j):
            arrived(q, item)
            to_side(q, item).start()

    def aside(q, j):
        for item in items_of(j):
            arrived(4 + q, item)

    for j in range(chunks):
        for item in items_of(j):
            @pl.when(inner)
            def _():
                arrived(0, item)
                to_over(0, item).start()
                to_side(0, item).start()
                arrived(8, item)

            @pl.when(outer)
            def _():
                arrived(2, item)
                to_side(2, item).start()

        if j + 2 < chunks:
            send_own(j + 2)
        else:
            second_wave(j + 2 - chunks)
            give_sparse(j + 2 - chunks).start()
        if j > 0:
            pass_aside(1, j - 1)

    for j in range(chunks):
        aside(0, j)
    use_own(0, 1)

    for j in range(chunks):
        @pl.when(inner)
        def _():
            for item in items_of(j):
                arrived(2, item)
                to_over(2, item).start()
                to_side(2, item).start()

        if j + 2 < chunks:
            second_wave(j + 2)
        else:
            give_sparse(j).start()
        if j == 0:
            pass_aside(1, last)
            for i in range(chunks):
                aside(1, i)
            use_own(1, 1)
        else:
            pass_aside(3, j - 1)
        if j == 1:
            take_sparse(0)
            use_other(0, 1, 0, 2)
        if j == 2:
            for i in range(2):
                aside(2, i)
            use_own(2, 1, 0, half)
    for j in range(2, chunks):
        aside(2, j)
    use_own(2, 1, half)
    use_other(0, 1, 2, 1)
    pass_aside(3, last)
    take_sparse(1)
    use_other(1, 2, 0, 3)
    for j in range(chunks):
        aside(3, j)
    use_own(3, 1)
    use_other(0, 2, 3, 1)
    give_back(0)
    give_back(1)

    lanes = lax.broadcasted_iota(jnp.int32, (1, LANES), 1) // 16
    mine = jnp.zeros((1, LANES), jnp.float32)
    for slot in range(8):
        mine += jnp.where(lanes == slot, metas[slot, 3:4, 0:LANES], 0.0)
    row_energies[0] = jnp.broadcast_to(mine, (8, LANES))
    give_energies.start()

    def finish(rounded, energies, at_z, at_inner):
        other_z = at_z + 1 - 2 * (at_z % 2)
        near = at_z + at_inner * (3 - 2 * at_z)
        far = other_z + at_inner * (3 - 2 * other_z)
        turned = rounded.T
        for slot in range(8):
            q = slot % 4
            from_z = near if q < 2 else far
            from_y = y if q % 2 == 0 else 1 - y
            from_core = core if slot < 4 else 1 - core
            design_ref[from_z * 4 + from_y * 2 + from_core] = turned[
                16 * slot:16 * slot + n_conf, 0:n_sparse
            ].astype(jnp.bfloat16)
        return jnp.sum((rounded * energies).T, axis=0, keepdims=True)[:, 0:n_sparse]

    take_sparse(2)
    take_sparse(3)
    use_other(2, 4, 0, 4)
    give_back(2)
    give_back(3)
    rhs_ref[...] = finish(
        sum_own[...].astype(jnp.bfloat16).astype(jnp.float32), mine, z, inner_i
    )

    give_energies.wait_recv()
    for part in range(len(cuts) - 1):
        give_sums(part).wait_recv()
    rhs_ref[...] += finish(
        in_other[...].astype(jnp.float32), row_energies[1, 0:1, :], pair_z, 1 - inner_i
    )

    give_energies.wait_send()
    for part in range(len(cuts) - 1):
        give_sparse(part).wait_send()
        give_sums(part).wait_send()
    for item in items:
        to_part(item).wait_send()
        for q in range(4):
            to_side(q, item).wait_send()
        to_over(0, item).wait_send()
        to_over(2, item).wait_send()

        @pl.when(inner)
        def _():
            to_cross(own, 0, item).wait_send()
            to_cross(8, 2, item).wait_send()


def split_both(descriptors, sparse_points, counts, energies):
    n_atoms, depth = descriptors.shape
    n_sparse = sparse_points.shape[0]
    n_conf = counts.shape[1]
    n_env = 16
    chunks = 4
    unit = n_sparse // 6 // LANES * LANES
    cuts = (0, 2 * unit, 4 * unit, 5 * unit, n_sparse)
    parts = len(cuts) - 1
    wide = pl.cdiv(n_sparse, LANES) * LANES
    dma = pltpu.SemaphoreType.DMA
    design, rhs = pl.pallas_call(
        functools.partial(block_kernel, cuts, chunks),
        out_shape=(
            jax.ShapeDtypeStruct((n_env, n_conf, n_sparse), jnp.bfloat16),
            jax.ShapeDtypeStruct((1, n_sparse), jnp.float32),
        ),
        in_specs=[pl.BlockSpec(memory_space=pltpu.HBM)] * 4,
        out_specs=(
            pl.BlockSpec(memory_space=pltpu.VMEM),
            pl.BlockSpec(memory_space=pltpu.VMEM),
        ),
        scratch_shapes=[
            pltpu.VMEM((10, n_atoms, depth), jnp.bfloat16),
            pltpu.VMEM((10, 8, n_atoms), jnp.float32),
            pltpu.VMEM((n_sparse, depth), jnp.bfloat16),
            pltpu.VMEM((n_sparse, depth), jnp.bfloat16),
            pltpu.VMEM((n_sparse, LANES), jnp.float32),
            pltpu.VMEM((n_sparse, LANES), jnp.float32),
            pltpu.VMEM((wide, LANES), jnp.float32),
            pltpu.VMEM((wide, LANES), jnp.float32),
            pltpu.VMEM((n_sparse, LANES), jnp.bfloat16),
            pltpu.VMEM((wide, LANES), jnp.bfloat16),
            pltpu.VMEM((2, 8, LANES), jnp.float32),
            pltpu.VMEM((1, n_conf), jnp.int32),
            pltpu.VMEM((1, n_conf), jnp.float32),
            dma((chunks,)),
            dma((3,)),
            dma((9, chunks + 1)),
            dma((2, chunks + 1)),
            dma((4, chunks + 1)),
            dma((chunks + 1,)),
            dma((2, chunks + 1)),
            dma((parts,)),
            dma((parts,)),
            dma((parts,)),
            dma((parts,)),
            dma,
            dma,
        ],
        compiler_params=pltpu.CompilerParams(
            collective_id=0, has_side_effects=True, vmem_limit_bytes=VMEM_BUDGET
        ),
        cost_estimate=pl.CostEstimate(
            flops=2 * n_env * n_atoms * n_sparse * depth,
            bytes_accessed=2 * (n_atoms + n_sparse) * depth,
            transcendentals=0,
        ),
    )(descriptors, sparse_points, counts, energies.reshape(1, n_conf))
    return (design.reshape(n_env * n_conf, n_sparse), rhs.reshape(n_sparse))


def solution(mesh):
    n_env = mesh.shape["env"]

    def on_device(descriptors, sparse_points, counts, energies):
        if n_env == 16 and counts.shape[1] <= 16 and sparse_points.shape[0] >= 6 * LANES:
            return split_both(descriptors, sparse_points, counts, energies)
        return gather_sparse(descriptors, sparse_points, counts, energies)

    return jax.shard_map(
        on_device,
        mesh=mesh,
        in_specs=(
            P(("group", "env"), None),
            P(("group", "env"), None),
            P(("group", "env"), None),
            P(("group", "env")),
        ),
        out_specs=(P("group", "env"), P(("group", "env"))),
        check_vma=False,
    )
```

```python
import functools

import jax
import jax.numpy as jnp
from jax import lax
from jax.experimental import pallas as pl
from jax.experimental.pallas import tpu as pltpu
from jax.sharding import PartitionSpec as P

EPS = 1e-06
LANES = 128
VMEM_BUDGET = 60 * 1024 * 1024


def inverse_norms(values):
    values_f = values.astype(jnp.float32)
    return lax.rsqrt(jnp.sum(values_f * values_f, axis=1) + EPS)


def kernel_block(atom_rows, inv_atoms, sparse_rows, inv_sparse):
    products = lax.dot_general(
        atom_rows, sparse_rows, (((1,), (1,)), ((), ())), preferred_element_type=jnp.float32
    )
    cosine = products * inv_atoms[:, None] * inv_sparse[None, :]
    squared = cosine * cosine
    return squared * squared


def gather_sparse(descriptors, sparse_points, counts, energies):
    atoms_here = descriptors.shape[0]
    all_energies = lax.all_gather(energies, "env", axis=0, tiled=True)
    inv_atoms = inverse_norms(descriptors)
    seg_ends = jnp.cumsum(counts[0])
    seg_starts = seg_ends - counts[0]
    positions = jnp.arange(atoms_here, dtype=jnp.int32)
    onehot = (
        (positions[None, :] >= seg_starts[:, None]) & (positions[None, :] < seg_ends[:, None])
    ).astype(jnp.float32)
    block_rows = lax.all_gather(sparse_points, "env", axis=0, tiled=True)
    inv_sparse = inverse_norms(block_rows)
    kernel = kernel_block(descriptors, inv_atoms, block_rows, inv_sparse)
    config_part = jnp.dot(onehot, kernel, precision=lax.Precision.HIGHEST)
    design = lax.all_to_all(
        config_part.astype(jnp.bfloat16), "env", split_axis=1, concat_axis=0, tiled=True
    )
    normal_rhs = jnp.dot(all_energies, design.astype(jnp.float32), precision=lax.Precision.HIGHEST)
    return (design, normal_rhs)


def block_kernel(
    cuts, chunks, a_hbm, s_hbm, counts_hbm, energies_hbm, design_ref, rhs_ref,
    blocks, metas, sparse, other, inv_own, inv_other, sum_own, sum_other, out_other, in_other,
    row_energies, counts_ref, energies_ref,
    own_sem, small_sem, recv, send_y, send_side, send_part, send_cross,
    s_send, s_recv, r_send, r_recv, e_send, e_recv,
):
    n_atoms, depth = a_hbm.shape
    n_sparse = s_hbm.shape[0]
    n_conf = counts_hbm.shape[1]
    rows = n_atoms // chunks
    half = n_atoms // 2
    META = chunks
    items = [0, META] + list(range(1, chunks))
    last = chunks - 1
    ahead = chunks // 2
    quarter = chunks // 4

    me = lax.axis_index("env")
    core = me % 2
    y = (me // 2) % 2
    z = me // 4
    inner_i = (z % 3 + 1) // 2
    inner = inner_i == 1
    outer = inner_i == 0
    pair_z = z + 1 - 2 * (z % 2)
    side = me + 1 - 2 * core
    over = me + 2 - 4 * y
    partner = pair_z * 4 + y * 2 + core
    cross = (3 - z) * 4 + y * 2 + core
    own = 9 * inner_i

    barrier = pltpu.get_barrier_semaphore()

    def greet(device):
        pl.semaphore_signal(
            barrier, inc=1, device_id={"env": device}, device_id_type=pl.DeviceIdType.MESH
        )

    for device in (side, over, partner):
        greet(device)

    @pl.when(inner)
    def _():
        greet(cross)

    def piece(slot, item):
        if item == META:
            return metas.at[slot]
        return blocks.at[slot, pl.ds(item * rows, rows)]

    def remote(src, dst, send, arrive, device):
        return pltpu.make_async_remote_copy(
            src_ref=src, dst_ref=dst, send_sem=send, recv_sem=arrive,
            device_id={"env": device}, device_id_type=pl.DeviceIdType.MESH,
        )

    def hand(src, dst, item, send, device):
        return remote(piece(src, item), piece(dst, item), send.at[item], recv.at[dst, item], device)

    def hand_own(dst, item, send, device):
        here = metas.at[own] if item == META else a_hbm.at[pl.ds(item * rows, rows)]
        return remote(here, piece(dst, item), send.at[item], recv.at[dst, item], device)

    def to_side(q, item):
        return hand(q, 4 + q, item, send_side.at[q], side)

    def to_over(q, item):
        return hand(q, q + 1, item, send_y.at[q // 2], over)

    def to_part(item):
        return hand_own(8 - 6 * inner_i, item, send_part, partner)

    def to_cross(src, dst, item):
        return hand(src, dst, item, send_cross.at[dst // 2], cross)

    def arrived(slot, item):
        remote(
            piece(slot, item), piece(slot, item), send_part.at[item], recv.at[slot, item], side
        ).wait_recv()

    def s_rows(n):
        return pl.ds(cuts[n], cuts[n + 1] - cuts[n])

    def give_sparse(n):
        return remote(s_hbm.at[s_rows(n)], other.at[s_rows(n)], s_send.at[n], s_recv.at[n], partner)

    def give_sums(n):
        return remote(
            out_other.at[s_rows(n)], in_other.at[s_rows(n)], r_send.at[n], r_recv.at[n], partner
        )

    give_energies = remote(row_energies.at[0], row_energies.at[1], e_send, e_recv, partner)

    local = [
        pltpu.make_async_copy(a_hbm.at[pl.ds(j * rows, rows)], piece(own, j), own_sem.at[j])
        for j in range(chunks)
    ]
    local_sparse = pltpu.make_async_copy(s_hbm, sparse, small_sem.at[0])
    local_counts = pltpu.make_async_copy(counts_hbm, counts_ref, small_sem.at[1])
    local_energies = pltpu.make_async_copy(energies_hbm, energies_ref, small_sem.at[2])
    for copy in local + [local_counts, local_energies, local_sparse]:
        copy.start()

    def send_own(item):
        to_part(item).start()

        @pl.when(inner)
        def _():
            hand_own(0, item, send_cross.at[0], cross).start()

        @pl.when(outer)
        def _():
            hand_own(1, item, send_y.at[0], over).start()
            hand_own(4, item, send_side.at[0], side).start()

    pl.semaphore_wait(barrier, 3 + inner_i)
    give_sparse(0).start()
    for item in range(ahead - 1):
        send_own(item)

    for copy in local:
        copy.wait()
    ones = jnp.ones((8, depth), jnp.bfloat16)
    contract = (((1,), (1,)), ((), ()))
    for j in range(2):
        values = blocks[own, j * half:(j + 1) * half, :].astype(jnp.float32)
        squares = values * values
        high = squares.astype(jnp.bfloat16)
        low = (squares - high.astype(jnp.float32)).astype(jnp.bfloat16)
        total = lax.dot_general(ones, high, contract, preferred_element_type=jnp.float32)
        total += lax.dot_general(ones, low, contract, preferred_element_type=jnp.float32)
        metas[own, :, j * half:(j + 1) * half] = lax.rsqrt(total + EPS)
    local_counts.wait()
    local_energies.wait()
    down = lax.broadcasted_iota(jnp.int32, (LANES, LANES), 0)
    along = lax.broadcasted_iota(jnp.int32, (LANES, LANES), 1) % 16
    blank = jnp.zeros((1, LANES - n_conf), jnp.float32)

    def spread(row, keep):
        keep = jnp.where(keep & (along < n_conf), 1.0, 0.0)
        return jnp.dot(
            jnp.broadcast_to(jnp.concatenate([row, blank], axis=1), (8, LANES)), keep,
            precision=lax.Precision.HIGHEST, preferred_element_type=jnp.float32,
        )[0:1]

    counts_f = counts_ref[...].astype(jnp.float32)
    metas[own, 1:2, 0:LANES] = spread(counts_f, down < along)
    metas[own, 2:3, 0:LANES] = spread(counts_f, down <= along)
    metas[own, 3:4, 0:LANES] = spread(energies_ref[...], down == along)
    send_own(META)
    send_own(ahead - 1)

    def scale_rows(points, inv, start, stop):
        values = points[start:stop, :].astype(jnp.float32)
        norms = lax.rsqrt(jnp.sum(values * values, axis=1, keepdims=True) + EPS)
        inv[start:stop, :] = jnp.broadcast_to(norms, (stop - start, LANES))

    local_sparse.wait()
    scale_rows(sparse, inv_own, 0, n_sparse)
    sum_own[...] = jnp.zeros_like(sum_own)
    sum_other[...] = jnp.zeros_like(sum_other)
    if in_other.shape[0] > n_sparse:
        in_other[n_sparse:, :] = jnp.zeros((in_other.shape[0] - n_sparse, LANES), jnp.bfloat16)

    def unit(points, inv, sums, start, stop, slot, first, end):
        products = lax.dot_general(
            points[start:stop, :], blocks[slot, first:end, :], contract,
            preferred_element_type=jnp.float32,
        )
        scale = jnp.concatenate([inv[start:stop, :]] * ((end - first) // LANES), axis=1)
        cosine = products * metas[slot, 0:1, first:end] * scale
        squared = cosine * cosine
        kernel = squared * squared
        high = kernel.astype(jnp.bfloat16)
        low = (kernel - high.astype(jnp.float32)).astype(jnp.bfloat16)
        at = (lax.broadcasted_iota(jnp.int32, (end - first, LANES), 0) + first).astype(jnp.float32)
        lane = lax.broadcasted_iota(jnp.int32, (end - first, LANES), 1)
        inside = (at >= metas[slot, 1:2, 0:LANES]) & (at < metas[slot, 2:3, 0:LANES])
        onehot = jnp.where(inside & (lane // 16 == slot), 1.0, 0.0).astype(jnp.bfloat16)
        total = jnp.dot(high, onehot, preferred_element_type=jnp.float32)
        total += jnp.dot(low, onehot, preferred_element_type=jnp.float32)
        sums[start:stop, :] += total

    def use_own(q, n, first=0, end=None):
        stop = n_atoms if end is None else end

        @pl.loop(0, 2 * n)
        def _(i):
            unit(sparse, inv_own, sum_own, 0, n_sparse, q + i // 2 + 4 * (i % 2), first, stop)

    def use_other(part, upto, q, n):
        @pl.loop(0, 2 * n)
        def _(i):
            unit(
                other, inv_other, sum_other, cuts[part], cuts[upto], q + i // 2 + 4 * (i % 2),
                0, n_atoms,
            )

    def take_sparse(part):
        give_sparse(part).wait_recv()
        scale_rows(other, inv_other, cuts[part], cuts[part + 1])

    def give_back(part):
        out_other[s_rows(part)] = sum_other[s_rows(part)].astype(jnp.bfloat16)
        give_sums(part).start()

    def items_of(j):
        return [0, META] if j == 0 else [j]

    def second_wave(j):
        for item in items_of(j):
            @pl.when(inner)
            def _():
                arrived(8, item)
                to_cross(8, 2, item).start()

            @pl.when(outer)
            def _():
                arrived(2, item)
                to_over(2, item).start()
                to_side(2, item).start()

    def pass_aside(q, j):
        for item in items_of(j):
            arrived(q, item)
            to_side(q, item).start()

    def aside(q, j):
        for item in items_of(j):
            arrived(4 + q, item)

    for j in range(chunks):
        for item in items_of(j):
            @pl.when(inner)
            def _():
                arrived(0, item)
                to_over(0, item).start()
                to_side(0, item).start()

        if j + ahead < chunks:
            send_own(j + ahead)
        else:
            second_wave(j + ahead - chunks)
        if j == 3 * quarter:
            give_sparse(1).start()
        if j > 0:
            pass_aside(1, j - 1)

    for j in range(chunks):
        aside(0, j)
    use_own(0, 1)

    for j in range(chunks):
        @pl.when(inner)
        def _():
            for item in items_of(j):
                arrived(2, item)
                to_over(2, item).start()
                to_side(2, item).start()

        if j + ahead < chunks:
            second_wave(j + ahead)
        if j == quarter:
            give_sparse(2).start()
        if j == 2 * quarter:
            give_sparse(3).start()
        if j == 0:
            pass_aside(1, last)
            for i in range(chunks):
                aside(1, i)
            use_own(1, 1)
        else:
            pass_aside(3, j - 1)
        if j == chunks // 2 - 1:
            take_sparse(0)
            use_other(0, 1, 0, 2)
        if j == 3 * quarter - 1:
            for i in range(chunks // 2):
                aside(2, i)
            use_own(2, 1, 0, half)
    for j in range(chunks // 2, chunks):
        aside(2, j)
    use_own(2, 1, half)
    take_sparse(1)
    use_other(1, 2, 0, 2)
    pass_aside(3, last)
    use_other(0, 2, 2, 1)
    for j in range(chunks):
        aside(3, j)
    use_own(3, 1)
    use_other(0, 2, 3, 1)
    give_back(0)
    give_back(1)

    lanes = lax.broadcasted_iota(jnp.int32, (1, LANES), 1) // 16
    mine = jnp.zeros((1, LANES), jnp.float32)
    for slot in range(8):
        mine += jnp.where(lanes == slot, metas[slot, 3:4, 0:LANES], 0.0)
    row_energies[0] = jnp.broadcast_to(mine, (8, LANES))
    give_energies.start()

    def finish(rounded, energies, at_z, at_inner):
        other_z = at_z + 1 - 2 * (at_z % 2)
        near = at_z + at_inner * (3 - 2 * at_z)
        far = other_z + at_inner * (3 - 2 * other_z)
        turned = rounded.T
        for slot in range(8):
            q = slot % 4
            from_z = near if q < 2 else far
            from_y = y if q % 2 == 0 else 1 - y
            from_core = core if slot < 4 else 1 - core
            design_ref[from_z * 4 + from_y * 2 + from_core] = turned[
                16 * slot:16 * slot + n_conf, 0:n_sparse
            ].astype(jnp.bfloat16)
        return jnp.sum((rounded * energies).T, axis=0, keepdims=True)[:, 0:n_sparse]

    take_sparse(2)
    take_sparse(3)
    use_other(2, 4, 0, 4)
    give_back(2)
    give_back(3)
    rhs_ref[...] = finish(
        sum_own[...].astype(jnp.bfloat16).astype(jnp.float32), mine, z, inner_i
    )

    give_energies.wait_recv()
    for part in range(len(cuts) - 1):
        give_sums(part).wait_recv()
    rhs_ref[...] += finish(
        in_other[...].astype(jnp.float32), row_energies[1, 0:1, :], pair_z, 1 - inner_i
    )

    give_energies.wait_send()
    for part in range(len(cuts) - 1):
        give_sparse(part).wait_send()
        give_sums(part).wait_send()
    for item in items:
        to_part(item).wait_send()
        for q in range(4):
            to_side(q, item).wait_send()
        to_over(0, item).wait_send()
        to_over(2, item).wait_send()

        @pl.when(inner)
        def _():
            hand_own(0, item, send_cross.at[0], cross).wait_send()
            to_cross(8, 2, item).wait_send()


def split_both(descriptors, sparse_points, counts, energies):
    n_atoms, depth = descriptors.shape
    n_sparse = sparse_points.shape[0]
    n_conf = counts.shape[1]
    n_env = 16
    chunks = 4
    unit = n_sparse // 6 // LANES * LANES
    cuts = (0, 2 * unit, 4 * unit, 5 * unit, n_sparse)
    parts = len(cuts) - 1
    wide = pl.cdiv(n_sparse, LANES) * LANES
    dma = pltpu.SemaphoreType.DMA
    design, rhs = pl.pallas_call(
        functools.partial(block_kernel, cuts, chunks),
        out_shape=(
            jax.ShapeDtypeStruct((n_env, n_conf, n_sparse), jnp.bfloat16),
            jax.ShapeDtypeStruct((1, n_sparse), jnp.float32),
        ),
        in_specs=[pl.BlockSpec(memory_space=pltpu.HBM)] * 4,
        out_specs=(
            pl.BlockSpec(memory_space=pltpu.VMEM),
            pl.BlockSpec(memory_space=pltpu.VMEM),
        ),
        scratch_shapes=[
            pltpu.VMEM((10, n_atoms, depth), jnp.bfloat16),
            pltpu.VMEM((10, 8, n_atoms), jnp.float32),
            pltpu.VMEM((n_sparse, depth), jnp.bfloat16),
            pltpu.VMEM((n_sparse, depth), jnp.bfloat16),
            pltpu.VMEM((n_sparse, LANES), jnp.float32),
            pltpu.VMEM((n_sparse, LANES), jnp.float32),
            pltpu.VMEM((wide, LANES), jnp.float32),
            pltpu.VMEM((wide, LANES), jnp.float32),
            pltpu.VMEM((n_sparse, LANES), jnp.bfloat16),
            pltpu.VMEM((wide, LANES), jnp.bfloat16),
            pltpu.VMEM((2, 8, LANES), jnp.float32),
            pltpu.VMEM((1, n_conf), jnp.int32),
            pltpu.VMEM((1, n_conf), jnp.float32),
            dma((chunks,)),
            dma((3,)),
            dma((9, chunks + 1)),
            dma((2, chunks + 1)),
            dma((4, chunks + 1)),
            dma((chunks + 1,)),
            dma((2, chunks + 1)),
            dma((parts,)),
            dma((parts,)),
            dma((parts,)),
            dma((parts,)),
            dma,
            dma,
        ],
        compiler_params=pltpu.CompilerParams(
            collective_id=0, has_side_effects=True, vmem_limit_bytes=VMEM_BUDGET
        ),
        cost_estimate=pl.CostEstimate(
            flops=2 * n_env * n_atoms * n_sparse * depth,
            bytes_accessed=2 * (n_atoms + n_sparse) * depth,
            transcendentals=0,
        ),
    )(descriptors, sparse_points, counts, energies.reshape(1, n_conf))
    return (design.reshape(n_env * n_conf, n_sparse), rhs.reshape(n_sparse))


def solution(mesh):
    n_env = mesh.shape["env"]

    def on_device(descriptors, sparse_points, counts, energies):
        if n_env == 16 and counts.shape[1] <= 16 and sparse_points.shape[0] >= 6 * LANES:
            return split_both(descriptors, sparse_points, counts, energies)
        return gather_sparse(descriptors, sparse_points, counts, energies)

    return jax.shard_map(
        on_device,
        mesh=mesh,
        in_specs=(
            P(("group", "env"), None),
            P(("group", "env"), None),
            P(("group", "env"), None),
            P(("group", "env")),
        ),
        out_specs=(P("group", "env"), P(("group", "env"))),
        check_vma=False,
    )
```
